32 devices in a mesh: fsdp: 2 (over core), context: 4 (over y, x), tensor: 4 (over z).
Axes of the slice: x: 2, y: 2, z: 4, core: 2. Of those that a mesh axis runs over, the one named last changes fastest.
Arguments:
- tokens: bfloat16 [8, 2048, 768], P('fsdp', ('context', 'tensor')), may hold values from -6 to 6
- segment_ids: int32 [8, 2048], P('fsdp'), may hold values from 0 to 14, never falling along the last dimension, each value on 1 to 800 neighbouring positions
- first_gain: bfloat16 [768], P(('fsdp', 'context')), may hold values from 0.25 to 1.75
- second_gain: bfloat16 [768], P(('fsdp', 'context')), may hold values from 0.25 to 1.75
- triple_weight: bfloat16 [768, 2304], P(('fsdp', 'context')), may hold values from -0.21875 to 0.21875
- mixing_weight: bfloat16 [768, 768], P(('fsdp', 'context')), may hold values from -0.875 to 0.875
- inner_weight: bfloat16 [768, 2, 1152], P(('fsdp', 'context'), None, 'tensor'), may hold values from -0.21875 to 0.21875
- outer_weight: bfloat16 [1152, 768], P('tensor', ('fsdp', 'context')), may hold values from -0.25 to 0.25
- cotangent: bfloat16 [8, 2048, 768], P('fsdp', ('context', 'tensor')), may hold values from -6 to 6
Outputs:
- outputs: bfloat16 [8, 2048, 768], P('fsdp', ('context', 'tensor'))
- input_gradient: float32 [8, 2048, 768], P('fsdp', ('context', 'tensor'))
- first_gradient: float32 [768], P(('fsdp', 'context'))
- second_gradient: float32 [768], P(('fsdp', 'context'))
- triple_gradient: float32 [768, 2304], P(('fsdp', 'context'))
- mixing_gradient: float32 [768, 768], P(('fsdp', 'context'))
- inner_gradient: float32 [768, 2, 1152], P(('fsdp', 'context'), None, 'tensor')
- outer_gradient: float32 [1152, 768], P('tensor', ('fsdp', 'context'))
The draws below stay inside these ranges and needn't reach their ends.
Inputs may be any that keep to these rules, and one draw needn't show every extreme that they name: `segment_ids`: along each sequence the ids never fall; each document (a run of equal ids) has 1 to 800 tokens and one has exactly 800; every id from 0 to 14 occurs in every sequence.
All inputs are finite; a program needn't handle non-finite values.
Results may differ from the reference program's by a relative error of at most 0.018.
Values may be sent and summed in bfloat16 or wider, within the bound.
A program may use at most 128 MiB of HBM per device.

```python
import math
import jax
import jax.numpy as jnp
import numpy as np
from jax import lax

D = 768
H = 12
HD = 64
FF = 1152
SEQ_LEN = 2048
SEQS = 8
SEGS = 15
DOC_MOST = 800


def with_spikes(entries, rng, source, target, blocks, factor):
    def block_of(dim):
        return (jnp.arange(entries.shape[dim]) // (entries.shape[dim] // blocks)).reshape((-1,) + (1,) * (entries.ndim - 1 - dim))

    first = jax.random.permutation(rng, blocks)[block_of(target)]
    second = (block_of(target) + blocks // 2) % blocks
    return jnp.where((block_of(source) == first) | (block_of(source) == second), factor * entries, entries)


def levels(stream_key, extent, split, least, high):
    loudness = 1.0
    for position, blocks in split:
        heights = jax.random.uniform(jax.random.fold_in(jax.random.fold_in(stream_key, 6), position), (blocks,), jnp.float32, least / len(split), high / len(split))
        loudness = loudness * jnp.repeat(jnp.exp(heights), extent[position] // blocks).reshape((-1,) + (1,) * (len(extent) - 1 - position))
    return loudness


def split_up(amount, total, reach, slope):
    loads = [(1 << 20) // math.isqrt(grade ** slope) + 1 for grade in range(2, amount + 1)]
    rest, holding = total - reach - (amount - 1), [1] * (amount - 1)
    while rest > 0:
        movable = [i for i in range(amount - 1) if holding[i] < reach]
        whole, budget = sum([loads[i] for i in movable]), rest
        for i in movable:
            more = min(reach - holding[i], max(1, budget * loads[i] // whole), rest)
            holding[i] = holding[i] + more
            rest = rest - more
    return np.array([reach] + holding)


def uneven_parts(stream_key, count, total, most, skew):
    if count == 2:
        one = jax.random.randint(stream_key, (), max(1, total - most), min(most, total - 1) + 1)
        return jnp.stack([one, total - one])
    sizes = jnp.asarray(split_up(count, total, most, skew), jnp.int32)
    twos = (count - 1) // 2
    source_of, taker = sizes[1:1 + 2 * twos:2], sizes[2:2 + 2 * twos:2]
    margin = jnp.minimum(source_of - 1, most - taker)
    shifted = jax.random.randint(jax.random.fold_in(stream_key, 1), (twos,), 0, 1 << 20) % (margin + 1)
    sizes = sizes.at[1:1 + 2 * twos:2].set(source_of - shifted).at[2:2 + 2 * twos:2].set(taker + shifted)
    return sizes[jax.random.permutation(jax.random.fold_in(stream_key, 2), count)]


def scatter_about(key, extent, spread, most, shards=(), held_as=jnp.bfloat16):
    values = spread * jax.random.normal(key, extent, jnp.float32)
    if shards:
        values = values * levels(key, extent, shards, -0.22, 0.18)
    return jnp.clip(values, -most, most).astype(held_as)


def heavy_noise(stream_key, extent, deviation, limit, shards, heavy, kind=jnp.bfloat16):
    array = deviation * jax.random.normal(stream_key, extent, jnp.float32)
    if shards:
        array = array * levels(stream_key, extent, shards, -0.22, 0.18)
    return jnp.clip(with_spikes(array, jax.random.fold_in(stream_key, 3), *heavy), -limit, limit).astype(kind)


def setup_inputs(seed: int = 0) -> dict:
    arg_keys = jax.random.split(jax.random.key(seed), 10)
    return {
        "tokens": scatter_about(arg_keys[0], (SEQS, SEQ_LEN, D), 1.0, 6.0, ((0, 2), (1, 16))),
        "segment_ids": jax.vmap(lambda own: jnp.searchsorted(jnp.cumsum(uneven_parts(own, SEGS, SEQ_LEN, DOC_MOST, 1)), jnp.arange(SEQ_LEN), side="right"))(jax.random.split(arg_keys[1], SEQS)).reshape((SEQS, SEQ_LEN)).astype(jnp.int32),
        "first_gain": jnp.clip(1.0 + 0.15 * jax.random.normal(arg_keys[2], (D,), jnp.float32), 0.25, 1.75).astype(jnp.bfloat16),
        "second_gain": jnp.clip(1.0 + 0.15 * jax.random.normal(arg_keys[3], (D,), jnp.float32), 0.25, 1.75).astype(jnp.bfloat16),
        "triple_weight": scatter_about(arg_keys[4], (D, 3 * D), D ** -0.5, 0.21875, ((0, 8),)),
        "mixing_weight": scatter_about(arg_keys[5], (D, D), (D // 16) ** -0.5, 0.875, ((0, 8),)),
        "inner_weight": scatter_about(arg_keys[6], (D, 2, FF), D ** -0.5, 0.21875, ((0, 8), (2, 4))),
        "outer_weight": scatter_about(arg_keys[7], (FF, D), (FF // 2) ** -0.5, 0.25, ((0, 4), (1, 8))),
        "cotangent": heavy_noise(arg_keys[8], (SEQS, SEQ_LEN, D), 1.0, 6.0, ((0, 2), (1, 16)), (0, 2, 2, 2.0)),
    }


THETA = 160000.0
EPSILON = 1e-05
MASKED = -1e+30
HIGHEST = lax.Precision.HIGHEST

@jax.custom_vjp
def low(v):
    return lax.optimization_barrier(v.astype(jnp.bfloat16)).astype(jnp.float32)

@jax.custom_vjp
def low_back(v):
    return v

def low_keep(v):
    return (low(v), None)

def low_pass(kept, grad):
    return (grad,)

def back_keep(v):
    return (v, None)

def back_low(kept, grad):
    return (low(grad),)
low.defvjp(low_keep, low_pass)
low_back.defvjp(back_keep, back_low)

def layer_norm(values, gain_vec):
    average = lax.optimization_barrier(jnp.mean(values, axis=-1, keepdims=True))
    centred = values - average
    variance = lax.optimization_barrier(jnp.mean(centred * centred, axis=-1, keepdims=True))
    return centred * lax.rsqrt(variance + EPSILON) * gain_vec

def doc_positions(segments):
    token_index = jnp.arange(segments.shape[-1], dtype=jnp.int32)
    changed = (segments[..., 1:] != segments[..., :-1]).astype(jnp.int32)
    starts = jnp.concatenate([jnp.ones(segments.shape[:-1] + (1,), jnp.int32), changed], axis=-1)
    return token_index - lax.cummax(token_index * starts, axis=segments.ndim - 1)

def rope_tables(positions):
    half_width = HD // 2
    freqs = THETA ** (-(jnp.arange(half_width, dtype=jnp.float32) * (2.0 / HD)))
    angles = positions.astype(jnp.float32)[..., None] * freqs
    return (jnp.cos(angles), jnp.sin(angles))

def rotate(values, cosines, sines):
    half_width = values.shape[-1] // 2
    leading = values[..., :half_width]
    trailing = values[..., half_width:]
    cos_wide = cosines[..., None, :]
    sin_wide = sines[..., None, :]
    return jnp.concatenate([leading * cos_wide - trailing * sin_wide, trailing * cos_wide + leading * sin_wide], axis=-1)

def sequence_forward(residual, first_vec, second_vec, triple_mat, mixing_mat, inner_mat, outer_mat, segments, cosines, sines):
    length = residual.shape[0]
    normed_one = low(layer_norm(residual, first_vec))
    projected = low_back(jnp.dot(normed_one, triple_mat, precision=HIGHEST)).reshape(length, 3, H, HD)
    queries = low(low_back(rotate(projected[:, 0], cosines, sines)))
    keys = low(low_back(rotate(projected[:, 1], cosines, sines)))
    values = low(low_back(projected[:, 2]))
    block_rows = min(512, length)

    def block_attend(start):
        query_block = lax.dynamic_slice_in_dim(queries, start, block_rows, 0)
        query_ids = lax.dynamic_slice_in_dim(segments, start, block_rows, 0)
        allowed = (query_ids[:, None] == segments[None, :])[None]
        scores = low_back(jnp.einsum('qhd,khd->hqk', query_block, keys, precision=HIGHEST) * HD ** (-0.5))
        scores = jnp.where(allowed, scores, MASKED)
        probs_low = low(jax.nn.softmax(scores, axis=-1))
        return jnp.einsum('hqk,khd->qhd', probs_low, values, precision=HIGHEST)
    block_starts = jnp.arange(0, length, block_rows, dtype=jnp.int32)
    attended = lax.map(jax.checkpoint(block_attend), block_starts).reshape(length, H * HD)
    attended = low(low_back(attended))
    middle = residual + low_back(jnp.dot(attended, mixing_mat, precision=HIGHEST))
    normed_two = low(layer_norm(middle, second_vec))
    gate_up = low_back(jnp.einsum('ld,dgf->lgf', normed_two, inner_mat, precision=HIGHEST))
    hidden = low(jax.nn.gelu(gate_up[:, 0], approximate=False) * gate_up[:, 1])
    return middle + low_back(jnp.dot(hidden, outer_mat, precision=HIGHEST))

def reference(tokens, segment_ids, first_gain, second_gain, triple_weight, mixing_weight, inner_weight, outer_weight, cotangent):
    first_vec = first_gain.astype(jnp.float32)
    second_vec = second_gain.astype(jnp.float32)
    triple_mat = triple_weight.astype(jnp.float32)
    mixing_mat = mixing_weight.astype(jnp.float32)
    inner_mat = inner_weight.astype(jnp.float32)
    outer_mat = outer_weight.astype(jnp.float32)

    def one_sequence(carried, bundle):
        rows_in, segments, incoming = bundle
        cosines, sines = rope_tables(doc_positions(segments))

        def forward(residual, gain_a, gain_b, mat_a, mat_b, mat_c, mat_d):
            return sequence_forward(residual, gain_a, gain_b, mat_a, mat_b, mat_c, mat_d, segments, cosines, sines)
        produced, pull_back = jax.vjp(forward, rows_in.astype(jnp.float32), first_vec, second_vec, triple_mat, mixing_mat, inner_mat, outer_mat)
        pulled = pull_back(incoming.astype(jnp.float32))
        updated = tuple((running + piece for running, piece in zip(carried, pulled[1:])))
        return (updated, (produced.astype(jnp.bfloat16), pulled[0]))
    zeros = (jnp.zeros(first_vec.shape, jnp.float32), jnp.zeros(second_vec.shape, jnp.float32), jnp.zeros(triple_mat.shape, jnp.float32), jnp.zeros(mixing_mat.shape, jnp.float32), jnp.zeros(inner_mat.shape, jnp.float32), jnp.zeros(outer_mat.shape, jnp.float32))
    summed, (outputs, input_gradient) = lax.scan(one_sequence, zeros, (tokens, segment_ids, cotangent))
    return (outputs, input_gradient, summed[0], summed[1], summed[2], summed[3], summed[4], summed[5])
```

```python
import functools

import jax
import jax.numpy as jnp
from jax import lax
from jax.experimental import pallas as pl
from jax.experimental.pallas import tpu as pltpu
from jax.sharding import PartitionSpec as P

H = 12
HD = 64
THETA = 160000.0
EPSILON = 1e-05
MASKED = -1e30
BLOCK = 256
SCALE = HD ** (-0.5)

F32 = jnp.float32
BF16 = jnp.bfloat16


def dot(a, b, ca, cb):
    return lax.dot_general(a, b, (((ca,), (cb,)), ((), ())), preferred_element_type=F32)


def norm_parts(values):
    average = jnp.mean(values, axis=-1, keepdims=True)
    centred = values - average
    variance = jnp.mean(centred * centred, axis=-1, keepdims=True)
    inverse = lax.rsqrt(variance + EPSILON)
    return centred * inverse, inverse


def norm_back(grad, gain, xhat, inverse):
    u = grad * gain
    return inverse * (
        u
        - jnp.mean(u, axis=-1, keepdims=True)
        - xhat * jnp.mean(u * xhat, axis=-1, keepdims=True)
    )


def doc_positions(segments):
    token_index = jnp.arange(segments.shape[-1], dtype=jnp.int32)
    changed = (segments[1:] != segments[:-1]).astype(jnp.int32)
    starts = jnp.concatenate([jnp.ones((1,), jnp.int32), changed], axis=-1)
    return token_index - lax.cummax(token_index * starts, axis=0)


def forward_kernel(heads, lo_ref, hi_ref, q_ref, k_ref, v_ref, qid_ref, kid_ref, o_ref, l_ref):
    b = pl.program_id(0)
    qids = qid_ref[...]
    queries = [q_ref[h] * jnp.asarray(SCALE, BF16) for h in range(heads)]

    def step(j, carry):
        start = pl.multiple_of(j * BLOCK, BLOCK)
        same = kid_ref[pl.ds(start, BLOCK), :] == qids
        new = []
        for h in range(heads):
            peak, total, acc = carry[h]
            s = dot(k_ref[h, :, pl.ds(start, BLOCK)], queries[h], 0, 0)
            s = jnp.where(same, s, MASKED)
            peak_new = jnp.maximum(peak, jnp.max(s, axis=0, keepdims=True))
            fade = jnp.exp(peak - peak_new)
            p = jnp.exp(s - peak_new)
            total = total * fade + jnp.sum(p, axis=0, keepdims=True)
            acc = acc * fade + dot(v_ref[h, :, pl.ds(start, BLOCK)], p.astype(BF16), 1, 0)
            new.append((peak_new, total, acc))
        return tuple(new)

    first = tuple(
        (
            jnp.full((1, BLOCK), MASKED, F32),
            jnp.zeros((1, BLOCK), F32),
            jnp.zeros((HD, BLOCK), F32),
        )
        for _ in range(heads)
    )
    done = lax.fori_loop(lo_ref[b], hi_ref[b], step, first)
    for h in range(heads):
        peak, total, acc = done[h]
        o_ref[h] = (acc / total).astype(BF16)
        l_ref[h] = peak + jnp.log(total)


def attention_forward(q, k, v, row_ids, col_ids, lo, hi):
    heads, width, length = q.shape
    block = pl.BlockSpec((heads, width, BLOCK), lambda b, *_: (0, 0, b))
    whole = pl.BlockSpec((heads, width, length), lambda b, *_: (0, 0, 0))
    return pl.pallas_call(
        functools.partial(forward_kernel, heads),
        grid_spec=pltpu.PrefetchScalarGridSpec(
            num_scalar_prefetch=2,
            grid=(length // BLOCK,),
            in_specs=[
                block,
                whole,
                whole,
                pl.BlockSpec((1, BLOCK), lambda b, *_: (0, b)),
                pl.BlockSpec((length, 1), lambda b, *_: (0, 0)),
            ],
            out_specs=[block, pl.BlockSpec((heads, 1, BLOCK), lambda b, *_: (0, 0, b))],
        ),
        out_shape=[
            jax.ShapeDtypeStruct((heads, width, length), BF16),
            jax.ShapeDtypeStruct((heads, 1, length), F32),
        ],
        compiler_params=pltpu.CompilerParams(vmem_limit_bytes=40 * 1024 * 1024),
        cost_estimate=pl.CostEstimate(
            flops=4 * heads * width * length * length // 3,
            bytes_accessed=10 * heads * width * length,
            transcendentals=heads * length * length // 3,
        ),
        name="attention_forward",
    )(lo, hi, q, k, v, row_ids, col_ids)


def backward_kernel(
    heads, lo_ref, hi_ref, q_ref, do_ref, o_ref, l_ref, k_ref, v_ref, qid_ref, kid_ref,
    dq_ref, dk_ref, dv_ref, dq_sum, row_sum,
):
    b = pl.program_id(0)

    @pl.when(b == 0)
    def _():
        dq_sum[...] = jnp.zeros_like(dq_sum)
        for h in range(heads):
            row_sum[h] = jnp.sum(
                do_ref[h].astype(F32) * o_ref[h].astype(F32), axis=0, keepdims=True
            )

    kids = kid_ref[...]
    scaled = [k_ref[h] * jnp.asarray(SCALE, BF16) for h in range(heads)]
    keys = [s.T for s in scaled]
    values = [v_ref[h].T for h in range(heads)]

    def step(j, carry):
        at = pl.ds(pl.multiple_of(j * BLOCK, BLOCK), BLOCK)
        same = kids == qid_ref[:, at]
        new = []
        for h in range(heads):
            dk, dv = carry[h]
            q = q_ref[h, :, at]
            do = do_ref[h, :, at]
            s = dot(keys[h], q, 1, 0)
            s = jnp.where(same, s, MASKED)
            p = jnp.exp(s - l_ref[h, :, at])
            dp = dot(values[h], do, 1, 0)
            ds = (p * (dp - row_sum[h, :, at])).astype(BF16)
            dv = dv + dot(do, p.astype(BF16), 1, 1)
            dk = dk + dot(q, ds, 1, 1)
            dq_sum[h, :, at] += dot(scaled[h], ds, 1, 0)
            new.append((dk, dv))
        return tuple(new)

    zero = jnp.zeros((HD, BLOCK), F32)
    done = lax.fori_loop(lo_ref[b], hi_ref[b], step, tuple((zero, zero) for _ in range(heads)))
    for h in range(heads):
        dk, dv = done[h]
        dk_ref[h] = (dk * SCALE).astype(BF16)
        dv_ref[h] = dv.astype(BF16)

    @pl.when(b == pl.num_programs(0) - 1)
    def _():
        dq_ref[...] = dq_sum[...].astype(BF16)


def attention_backward(q, k, v, o, do, logsum, row_ids, col_ids, lo, hi):
    heads, width, length = q.shape
    block = pl.BlockSpec((heads, width, BLOCK), lambda b, *_: (0, 0, b))
    whole = pl.BlockSpec((heads, width, length), lambda b, *_: (0, 0, 0))
    shape = jax.ShapeDtypeStruct((heads, width, length), BF16)
    return pl.pallas_call(
        functools.partial(backward_kernel, heads),
        grid_spec=pltpu.PrefetchScalarGridSpec(
            num_scalar_prefetch=2,
            grid=(length // BLOCK,),
            in_specs=[
                whole,
                whole,
                whole,
                pl.BlockSpec((heads, 1, length), lambda b, *_: (0, 0, 0)),
                block,
                block,
                pl.BlockSpec((1, length), lambda b, *_: (0, 0)),
                pl.BlockSpec((BLOCK, 1), lambda b, *_: (b, 0)),
            ],
            out_specs=[whole, block, block],
            scratch_shapes=[
                pltpu.VMEM((heads, width, length), F32),
                pltpu.VMEM((heads, 1, length), F32),
            ],
        ),
        out_shape=[shape, shape, shape],
        compiler_params=pltpu.CompilerParams(vmem_limit_bytes=40 * 1024 * 1024),
        cost_estimate=pl.CostEstimate(
            flops=10 * heads * width * length * length // 3,
            bytes_accessed=16 * heads * width * length,
            transcendentals=heads * length * length // 3,
        ),
        name="attention_backward",
    )(lo, hi, q, do, o, logsum, k, v, row_ids, col_ids)


def gated_unit(gate_part, up_part):
    return jax.nn.gelu(gate_part, approximate=False) * up_part


def turn(values, cosines, sines):
    a, b = values[..., : HD // 2, :], values[..., HD // 2 :, :]
    return jnp.concatenate([a * cosines - b * sines, b * cosines + a * sines], axis=-2)


def per_device(
    tokens, segment_ids, first_gain, second_gain, triple_weight, mixing_weight,
    inner_weight, outer_weight, cotangent,
):
    cs = lax.axis_size("context")
    ts = lax.axis_size("tensor")
    fs = lax.axis_size("fsdp")
    t_rank = lax.axis_index("tensor")
    seqs, rows_in, width = tokens.shape
    assert seqs == ts
    length = segment_ids.shape[1]
    heads = H // cs
    span = heads * HD
    wrows = triple_weight.shape[0]
    units = inner_weight.shape[2]
    rows = rows_in * ts

    gains = jnp.stack([first_gain, second_gain], axis=1)
    gains = jnp.broadcast_to(jnp.pad(gains, ((0, 0), (0, 62)))[None], (cs, wrows, 64))
    columns = jnp.transpose(triple_weight.reshape(wrows, 3, cs, span), (2, 0, 1, 3))
    columns = jnp.concatenate([columns.reshape(cs, wrows, 3 * span), gains], axis=2)
    columns = lax.all_to_all(columns, "context", 0, 0, tiled=True).reshape(cs * wrows, -1)
    columns = lax.all_gather(columns, "fsdp", axis=0, tiled=True)
    w_own = columns[:, : 3 * span]
    gain_one = columns[:, 3 * span].astype(F32)
    gain_two = columns[:, 3 * span + 1].astype(F32)

    own = lax.all_to_all(tokens, "tensor", 0, 0, tiled=True).reshape(rows, width)
    residual = own.astype(F32)
    xhat_one, inverse_one = norm_parts(residual)
    normed_own = (xhat_one * gain_one).astype(BF16)
    normed_one = lax.all_gather(normed_own, "context", axis=0, tiled=True)

    mixing = lax.all_gather(mixing_weight, ("fsdp", "context"), axis=0, tiled=True)
    inner_all = lax.all_gather(inner_weight.reshape(wrows, 2 * units), ("fsdp", "context"), axis=0, tiled=True)
    outer_all = lax.all_gather(outer_weight.T, ("fsdp", "context"), axis=0, tiled=True)
    unit_all = lax.all_gather(
        jnp.concatenate([inner_all, outer_all], axis=1), "tensor", axis=0
    )
    unit_all = jnp.transpose(unit_all.reshape(ts, width, 3, units), (1, 2, 0, 3))
    unit_all = unit_all.reshape(width, 3 * ts * units)
    full = ts * units
    inner = unit_all[:, : 2 * full]
    outer_t = unit_all[:, 2 * full :]

    cot = lax.all_to_all(cotangent, "tensor", 0, 0, tiled=True).reshape(rows, width)

    segments = lax.dynamic_index_in_dim(segment_ids, t_rank, 0, keepdims=False)
    positions = doc_positions(segments)
    freqs = THETA ** (-(jnp.arange(HD // 2, dtype=F32) * (2.0 / HD)))
    angles = freqs[:, None] * positions.astype(F32)[None, :]
    cosines, sines = jnp.cos(angles), jnp.sin(angles)
    by_block = segments.reshape(length // BLOCK, BLOCK)
    low_at = jnp.sum(segments[None, :] < by_block[:, :1], axis=1, dtype=jnp.int32)
    high_at = jnp.sum(segments[None, :] <= by_block[:, -1:], axis=1, dtype=jnp.int32)
    lo = low_at // BLOCK
    hi = (high_at + BLOCK - 1) // BLOCK
    row_ids = segments.reshape(1, length)
    col_ids = segments.reshape(length, 1)

    projected = dot(w_own, normed_one, 0, 1).reshape(3, heads, HD, length)
    q = turn(projected[0], cosines, sines).astype(BF16)
    k = turn(projected[1], cosines, sines).astype(BF16)
    v = projected[2].astype(BF16)
    o, logsum = attention_forward(q, k, v, row_ids, col_ids, lo, hi)

    sent = jnp.transpose(o.reshape(span, cs, rows), (1, 0, 2))
    attended = lax.all_to_all(sent, "context", 0, 0, tiled=True).reshape(cs * span, rows)

    middle = residual + dot(attended, mixing, 0, 0)
    xhat_two, inverse_two = norm_parts(middle)
    normed_two = (xhat_two * gain_two).astype(BF16)
    gate_up = dot(normed_two, inner, 1, 0)
    hidden, unit_pull = jax.vjp(gated_unit, gate_up[:, :full], gate_up[:, full:])
    hidden = hidden.astype(BF16)
    outputs = (middle + dot(hidden, outer_t, 1, 1)).astype(BF16)
    grad_hidden = dot(cot, outer_t, 1, 0)
    grad_gate, grad_up = unit_pull(grad_hidden)
    grad_gate_up = jnp.concatenate([grad_gate, grad_up], axis=1).astype(BF16)
    grad_two = dot(grad_gate_up, inner, 1, 1)
    second_part = jnp.sum(grad_two * xhat_two, axis=0)
    grad_middle = cot.astype(F32) + norm_back(grad_two, gain_two, xhat_two, inverse_two)
    grad_mixed = grad_middle.astype(BF16)
    grad_att = dot(mixing, grad_mixed, 1, 1).astype(BF16)
    grad_att = lax.all_to_all(grad_att.reshape(cs, span, rows), "context", 0, 0, tiled=True)
    do = jnp.transpose(grad_att, (1, 0, 2)).reshape(heads, HD, length)

    unit_grad = jnp.concatenate(
        [dot(normed_two, grad_gate_up, 0, 0), dot(cot, hidden, 0, 0)], axis=1
    )
    unit_grad = jnp.transpose(unit_grad.reshape(width, 3, ts, units), (2, 0, 1, 3))
    unit_grad = unit_grad.astype(BF16).reshape(ts, width, 3 * units)
    unit_grad = lax.psum_scatter(unit_grad, "tensor", scatter_dimension=0, tiled=True)[0]
    unit_grad = lax.psum_scatter(unit_grad, ("fsdp", "context"), scatter_dimension=0, tiled=True)
    unit_grad = unit_grad.astype(F32)
    inner_gradient = unit_grad[:, : 2 * units].reshape(wrows, 2, units)
    outer_gradient = unit_grad[:, 2 * units :].T

    mix_grad = dot(attended, grad_mixed, 1, 0).reshape(fs * cs, wrows, width)
    extra = jnp.pad(second_part.reshape(fs * cs, 1, wrows), ((0, 0), (0, 15), (0, width - wrows)))
    mix_grad = jnp.concatenate([mix_grad, extra], axis=1).astype(BF16)
    mix_grad = lax.psum_scatter(mix_grad, ("fsdp", "context"), scatter_dimension=0, tiled=True)[0]
    mix_grad = lax.psum(mix_grad, "tensor").astype(F32)
    mixing_gradient = mix_grad[:wrows]
    second_gradient = mix_grad[wrows, :wrows]

    outputs = lax.all_to_all(outputs.reshape(ts, rows_in, width), "tensor", 0, 0, tiled=True)

    dq, dk, dv = attention_backward(q, k, v, o, do, logsum, row_ids, col_ids, lo, hi)
    grad_p = jnp.concatenate(
        [
            turn(dq.astype(F32), cosines, -sines).astype(BF16),
            turn(dk.astype(F32), cosines, -sines).astype(BF16),
            dv,
        ],
        axis=0,
    ).reshape(3 * span, length)
    grad_one = dot(grad_p, w_own, 0, 1).astype(BF16).reshape(cs, rows, width)
    grad_one = lax.all_to_all(grad_one, "context", 0, 0, tiled=True)
    grad_one = jnp.sum(grad_one.astype(F32), axis=0)
    input_gradient = grad_middle + norm_back(grad_one, gain_one, xhat_one, inverse_one)
    input_gradient = lax.all_to_all(
        input_gradient.astype(BF16).reshape(ts, rows_in, width), "tensor", 0, 0, tiled=True
    ).astype(F32)

    triple_grad = dot(normed_one, grad_p, 0, 1).astype(BF16).reshape(fs * cs, wrows, 3 * span)
    triple_grad = lax.all_to_all(triple_grad, ("fsdp", "context"), 0, 0, tiled=True)
    triple_grad = jnp.sum(triple_grad.reshape(fs, cs, wrows, 3, span).astype(F32), axis=0)
    triple_grad = lax.psum(triple_grad.astype(BF16), "tensor").astype(F32)
    triple_gradient = jnp.transpose(triple_grad, (1, 2, 0, 3)).reshape(wrows, 3 * width)
    first_gradient = jnp.sum(
        triple_gradient * triple_weight.astype(F32), axis=1
    ) / first_gain.astype(F32)
    return (
        outputs,
        input_gradient,
        first_gradient,
        second_gradient,
        triple_gradient,
        mixing_gradient,
        inner_gradient,
        outer_gradient,
    )


def solution(mesh):
    rows = P("fsdp", ("context", "tensor"), None)
    both = ("fsdp", "context")
    weights = (P(both), P(both), P(both, None), P(both, None), P(both, None, "tensor"), P("tensor", both))
    return jax.shard_map(
        per_device,
        mesh=mesh,
        in_specs=(rows, P("fsdp", None)) + weights + (rows,),
        out_specs=(rows, rows) + weights,
        check_vma=False,
    )
```

```python
import functools

import jax
import jax.numpy as jnp
from jax import lax
from jax.experimental import pallas as pl
from jax.experimental.pallas import tpu as pltpu
from jax.sharding import PartitionSpec as P

H = 12
HD = 64
THETA = 160000.0
EPSILON = 1e-05
MASKED = -1e30
BLOCK = 256
SCALE = HD ** (-0.5)

F32 = jnp.float32
BF16 = jnp.bfloat16


def dot(a, b, ca, cb):
    return lax.dot_general(a, b, (((ca,), (cb,)), ((), ())), preferred_element_type=F32)


def norm_parts(values):
    average = jnp.mean(values, axis=-1, keepdims=True)
    centred = values - average
    variance = jnp.mean(centred * centred, axis=-1, keepdims=True)
    inverse = lax.rsqrt(variance + EPSILON)
    return centred * inverse, inverse


def norm_back(grad, gain, xhat, inverse):
    u = grad * gain
    return inverse * (
        u
        - jnp.mean(u, axis=-1, keepdims=True)
        - xhat * jnp.mean(u * xhat, axis=-1, keepdims=True)
    )


def doc_positions(segments):
    token_index = jnp.arange(segments.shape[-1], dtype=jnp.int32)
    changed = (segments[1:] != segments[:-1]).astype(jnp.int32)
    starts = jnp.concatenate([jnp.ones((1,), jnp.int32), changed], axis=-1)
    return token_index - lax.cummax(token_index * starts, axis=0)


def forward_kernel(heads, lo_ref, hi_ref, q_ref, k_ref, v_ref, qid_ref, kid_ref, o_ref, l_ref):
    b = pl.program_id(0)
    qids = qid_ref[...]
    queries = [q_ref[h] * jnp.asarray(SCALE, BF16) for h in range(heads)]

    def step(j, carry):
        start = pl.multiple_of(j * BLOCK, BLOCK)
        same = kid_ref[pl.ds(start, BLOCK), :] == qids
        new = []
        for h in range(heads):
            peak, total, acc = carry[h]
            s = dot(k_ref[h, :, pl.ds(start, BLOCK)], queries[h], 0, 0)
            s = jnp.where(same, s, MASKED)
            peak_new = jnp.maximum(peak, jnp.max(s, axis=0, keepdims=True))
            fade = jnp.exp(peak - peak_new)
            p = jnp.exp(s - peak_new)
            total = total * fade + jnp.sum(p, axis=0, keepdims=True)
            acc = acc * fade + dot(v_ref[h, :, pl.ds(start, BLOCK)], p.astype(BF16), 1, 0)
            new.append((peak_new, total, acc))
        return tuple(new)

    first = tuple(
        (
            jnp.full((1, BLOCK), MASKED, F32),
            jnp.zeros((1, BLOCK), F32),
            jnp.zeros((HD, BLOCK), F32),
        )
        for _ in range(heads)
    )
    done = lax.fori_loop(lo_ref[b], hi_ref[b], step, first)
    for h in range(heads):
        peak, total, acc = done[h]
        o_ref[0, h] = (acc / total).astype(BF16)
        l_ref[h] = peak + jnp.log(total)


def attention_forward(q, k, v, row_ids, col_ids, lo, hi, parts):
    heads, width, length = q.shape
    per = length // parts // BLOCK
    block = pl.BlockSpec((heads, width, BLOCK), lambda b, *_: (0, 0, b))
    whole = pl.BlockSpec((heads, width, length), lambda b, *_: (0, 0, 0))
    return pl.pallas_call(
        functools.partial(forward_kernel, heads),
        grid_spec=pltpu.PrefetchScalarGridSpec(
            num_scalar_prefetch=2,
            grid=(length // BLOCK,),
            in_specs=[
                block,
                whole,
                whole,
                pl.BlockSpec((1, BLOCK), lambda b, *_: (0, b)),
                pl.BlockSpec((length, 1), lambda b, *_: (0, 0)),
            ],
            out_specs=[
                pl.BlockSpec((1, heads, width, BLOCK), lambda b, *_: (b // per, 0, 0, b % per)),
                pl.BlockSpec((heads, 1, BLOCK), lambda b, *_: (0, 0, b)),
            ],
        ),
        out_shape=[
            jax.ShapeDtypeStruct((parts, heads, width, length // parts), BF16),
            jax.ShapeDtypeStruct((heads, 1, length), F32),
        ],
        compiler_params=pltpu.CompilerParams(vmem_limit_bytes=40 * 1024 * 1024),
        cost_estimate=pl.CostEstimate(
            flops=4 * heads * width * length * length // 3,
            bytes_accessed=10 * heads * width * length,
            transcendentals=heads * length * length // 3,
        ),
        name="attention_forward",
    )(lo, hi, q, k, v, row_ids, col_ids)


def backward_kernel(
    heads, lo_ref, hi_ref, q_ref, do_ref, o_ref, l_ref, k_ref, v_ref, qid_ref, kid_ref,
    dq_ref, dk_ref, dv_ref, dq_sum, row_sum,
):
    b = pl.program_id(0)
    parts, _, _, rows = do_ref.shape
    per = rows // BLOCK

    @pl.when(b == 0)
    def _():
        dq_sum[...] = jnp.zeros_like(dq_sum)
        for c in range(parts):
            for h in range(heads):
                row_sum[h, :, c * rows : (c + 1) * rows] = jnp.sum(
                    do_ref[c, h].astype(F32) * o_ref[c, h].astype(F32), axis=0, keepdims=True
                )

    kids = kid_ref[...]
    scaled = [k_ref[h] * jnp.asarray(SCALE, BF16) for h in range(heads)]
    keys = [s.T for s in scaled]
    values = [v_ref[h].T for h in range(heads)]

    def step(j, carry):
        at = pl.ds(pl.multiple_of(j * BLOCK, BLOCK), BLOCK)
        same = kids == qid_ref[:, at]
        new = []
        for h in range(heads):
            dk, dv = carry[h]
            q = q_ref[h, :, at]
            do = do_ref[j // per, h, :, pl.ds(pl.multiple_of((j % per) * BLOCK, BLOCK), BLOCK)]
            s = dot(keys[h], q, 1, 0)
            s = jnp.where(same, s, MASKED)
            p = jnp.exp(s - l_ref[h, :, at])
            dp = dot(values[h], do, 1, 0)
            ds = (p * (dp - row_sum[h, :, at])).astype(BF16)
            dv = dv + dot(do, p.astype(BF16), 1, 1)
            dk = dk + dot(q, ds, 1, 1)
            dq_sum[h, :, at] += dot(scaled[h], ds, 1, 0)
            new.append((dk, dv))
        return tuple(new)

    zero = jnp.zeros((HD, BLOCK), F32)
    done = lax.fori_loop(lo_ref[b], hi_ref[b], step, tuple((zero, zero) for _ in range(heads)))
    for h in range(heads):
        dk, dv = done[h]
        dk_ref[h] = (dk * SCALE).astype(BF16)
        dv_ref[h] = dv.astype(BF16)

    @pl.when(b == pl.num_programs(0) - 1)
    def _():
        dq_ref[...] = dq_sum[...].astype(BF16)


def attention_backward(q, k, v, o, do, logsum, row_ids, col_ids, lo, hi):
    heads, width, length = q.shape
    block = pl.BlockSpec((heads, width, BLOCK), lambda b, *_: (0, 0, b))
    whole = pl.BlockSpec((heads, width, length), lambda b, *_: (0, 0, 0))
    spread = pl.BlockSpec(do.shape, lambda b, *_: (0, 0, 0, 0))
    shape = jax.ShapeDtypeStruct((heads, width, length), BF16)
    return pl.pallas_call(
        functools.partial(backward_kernel, heads),
        grid_spec=pltpu.PrefetchScalarGridSpec(
            num_scalar_prefetch=2,
            grid=(length // BLOCK,),
            in_specs=[
                whole,
                spread,
                spread,
                pl.BlockSpec((heads, 1, length), lambda b, *_: (0, 0, 0)),
                block,
                block,
                pl.BlockSpec((1, length), lambda b, *_: (0, 0)),
                pl.BlockSpec((BLOCK, 1), lambda b, *_: (b, 0)),
            ],
            out_specs=[whole, block, block],
            scratch_shapes=[
                pltpu.VMEM((heads, width, length), F32),
                pltpu.VMEM((heads, 1, length), F32),
            ],
        ),
        out_shape=[shape, shape, shape],
        compiler_params=pltpu.CompilerParams(vmem_limit_bytes=40 * 1024 * 1024),
        cost_estimate=pl.CostEstimate(
            flops=10 * heads * width * length * length // 3,
            bytes_accessed=16 * heads * width * length,
            transcendentals=heads * length * length // 3,
        ),
        name="attention_backward",
    )(lo, hi, q, do, o, logsum, k, v, row_ids, col_ids)


def gated_unit(gate_part, up_part):
    return jax.nn.gelu(gate_part, approximate=False) * up_part


def turn(values, cosines, sines):
    a, b = values[..., : HD // 2, :], values[..., HD // 2 :, :]
    return jnp.concatenate([a * cosines - b * sines, b * cosines + a * sines], axis=-2)


def gather(block, axis):
    count = lax.axis_size(axis)
    copies = jnp.broadcast_to(block[None], (count,) + block.shape)
    return lax.all_to_all(copies, axis, 0, 0, tiled=True)


def scatter_sum(blocks, axis):
    return jnp.sum(lax.all_to_all(blocks, axis, 0, 0, tiled=True).astype(F32), axis=0)


def per_device(
    tokens, segment_ids, first_gain, second_gain, triple_weight, mixing_weight,
    inner_weight, outer_weight, cotangent,
):
    cs = lax.axis_size("context")
    ts = lax.axis_size("tensor")
    fs = lax.axis_size("fsdp")
    t_rank = lax.axis_index("tensor")
    seqs, rows_in, width = tokens.shape
    assert seqs == ts and ts == cs
    length = segment_ids.shape[1]
    heads = H // cs
    span = heads * HD
    wrows = triple_weight.shape[0]
    units = inner_weight.shape[2]
    rows = rows_in * ts

    gains = jnp.stack([first_gain, second_gain], axis=1)
    gains = jnp.broadcast_to(jnp.pad(gains, ((0, 0), (0, 62)))[None], (cs, wrows, 64))
    columns = jnp.transpose(triple_weight.reshape(wrows, 3, cs, span), (2, 0, 1, 3))
    columns = jnp.concatenate([columns.reshape(cs, wrows, 3 * span), gains], axis=2)
    columns = lax.all_to_all(columns, "context", 0, 0, tiled=True).reshape(cs * wrows, -1)
    columns = lax.all_gather(columns, "fsdp", axis=0, tiled=True)
    w_own = columns[:, : 3 * span]
    gain_one = columns[:, 3 * span].astype(F32)
    gain_two = columns[:, 3 * span + 1].astype(F32)

    own = lax.all_to_all(tokens, "tensor", 0, 0, tiled=True).reshape(rows, width)
    residual = own.astype(F32)
    xhat_one, inverse_one = norm_parts(residual)
    normed_own = (xhat_one * gain_one).astype(BF16)
    normed_one = lax.all_gather(normed_own, "context", axis=0, tiled=True)

    full = ts * units
    unit_own = jnp.concatenate([inner_weight.reshape(wrows, 2 * units), outer_weight.T], axis=1)
    unit_all = gather(unit_own, "tensor").reshape(ts, wrows, 3, units)
    unit_all = jnp.transpose(unit_all, (1, 2, 0, 3)).reshape(wrows, 3 * full)
    packed = jnp.concatenate([unit_all, mixing_weight], axis=1)
    packed, normed_one = lax.optimization_barrier((packed, normed_one))
    packed = gather(packed, "context").reshape(cs * wrows, 3 * full + width)
    packed = gather(packed, "fsdp").reshape(width, 3 * full + width)
    inner = packed[:, : 2 * full]
    outer_t = packed[:, 2 * full : 3 * full]
    mixing = packed[:, 3 * full :]

    cot = lax.all_to_all(cotangent, "tensor", 0, 0, tiled=True).reshape(rows, width)

    segments = lax.dynamic_index_in_dim(segment_ids, t_rank, 0, keepdims=False)
    positions = doc_positions(segments)
    freqs = THETA ** (-(jnp.arange(HD // 2, dtype=F32) * (2.0 / HD)))
    angles = freqs[:, None] * positions.astype(F32)[None, :]
    cosines, sines = jnp.cos(angles), jnp.sin(angles)
    by_block = segments.reshape(length // BLOCK, BLOCK)
    low_at = jnp.sum(segments[None, :] < by_block[:, :1], axis=1, dtype=jnp.int32)
    high_at = jnp.sum(segments[None, :] <= by_block[:, -1:], axis=1, dtype=jnp.int32)
    lo = low_at // BLOCK
    hi = (high_at + BLOCK - 1) // BLOCK
    row_ids = segments.reshape(1, length)
    col_ids = segments.reshape(length, 1)

    projected = dot(w_own, normed_one, 0, 1).reshape(3, heads, HD, length)
    q = turn(projected[0], cosines, sines).astype(BF16)
    k = turn(projected[1], cosines, sines).astype(BF16)
    v = projected[2].astype(BF16)
    o, logsum = attention_forward(q, k, v, row_ids, col_ids, lo, hi, cs)

    sent = o.reshape(cs, span, rows)
    attended = lax.all_to_all(sent, "context", 0, 0, tiled=True).reshape(cs * span, rows)

    middle = residual + dot(attended, mixing, 0, 0)
    xhat_two, inverse_two = norm_parts(middle)
    normed_two = (xhat_two * gain_two).astype(BF16)
    gate_up = dot(normed_two, inner, 1, 0)
    hidden, unit_pull = jax.vjp(gated_unit, gate_up[:, :full], gate_up[:, full:])
    hidden = hidden.astype(BF16)
    outputs = (middle + dot(hidden, outer_t, 1, 1)).astype(BF16)
    grad_hidden = dot(cot, outer_t, 1, 0)
    grad_gate, grad_up = unit_pull(grad_hidden)
    grad_gate_up = jnp.concatenate([grad_gate, grad_up], axis=1).astype(BF16)
    grad_two = dot(grad_gate_up, inner, 1, 1)
    second_part = jnp.sum(grad_two * xhat_two, axis=0)
    grad_middle = cot.astype(F32) + norm_back(grad_two, gain_two, xhat_two, inverse_two)
    grad_mixed = grad_middle.astype(BF16)
    grad_att = dot(mixing, grad_mixed, 1, 1).astype(BF16)
    grad_att = lax.all_to_all(grad_att.reshape(cs, span, rows), "context", 0, 0, tiled=True)
    do = grad_att.reshape(cs, heads, HD, rows)

    second_wide = jnp.broadcast_to(second_part[:, None], (width, 128))
    weight_grad = jnp.concatenate(
        [
            dot(normed_two, grad_gate_up, 0, 0).astype(BF16),
            dot(cot, hidden, 0, 0).astype(BF16),
            dot(attended, grad_mixed, 1, 0).astype(BF16),
            second_wide.astype(BF16),
        ],
        axis=1,
    )
    lanes = 3 * full + width + 128
    weight_grad = scatter_sum(weight_grad.reshape(fs, cs * wrows, lanes), "fsdp").astype(BF16)
    weight_grad = scatter_sum(weight_grad.reshape(cs, wrows, lanes), "context").astype(BF16)
    unit_grad = jnp.transpose(weight_grad[:, : 3 * full].reshape(wrows, 3, ts, units), (2, 0, 1, 3))
    unit_grad = unit_grad.reshape(ts, wrows, 3 * units)
    other_grad = jnp.broadcast_to(weight_grad[None, :, 3 * full :], (ts, wrows, width + 128))
    weight_grad = scatter_sum(jnp.concatenate([other_grad, unit_grad], axis=2), "tensor")
    mixing_gradient = weight_grad[:, :width]
    second_gradient = weight_grad[:, width]
    unit_grad = weight_grad[:, width + 128 :]
    inner_gradient = unit_grad[:, : 2 * units].reshape(wrows, 2, units)
    outer_gradient = unit_grad[:, 2 * units :].T

    outputs = lax.all_to_all(outputs.reshape(ts, rows_in, width), "tensor", 0, 0, tiled=True)

    dq, dk, dv = attention_backward(q, k, v, o, do, logsum, row_ids, col_ids, lo, hi)
    grad_p = jnp.concatenate(
        [
            turn(dq.astype(F32), cosines, -sines).astype(BF16),
            turn(dk.astype(F32), cosines, -sines).astype(BF16),
            dv,
        ],
        axis=0,
    ).reshape(3 * span, length)
    grad_one = dot(grad_p, w_own, 0, 1).astype(BF16).reshape(cs, rows, width)
    grad_one = lax.all_to_all(grad_one, "context", 0, 0, tiled=True)
    grad_one = jnp.sum(grad_one.astype(F32), axis=0)
    input_gradient = grad_middle + norm_back(grad_one, gain_one, xhat_one, inverse_one)
    input_gradient = lax.all_to_all(
        input_gradient.astype(BF16).reshape(ts, rows_in, width), "tensor", 0, 0, tiled=True
    ).astype(F32)

    triple_grad = dot(normed_one, grad_p, 0, 1).astype(BF16).reshape(fs * cs, wrows, 3 * span)
    triple_grad = lax.all_to_all(triple_grad, ("fsdp", "context"), 0, 0, tiled=True)
    triple_grad = jnp.sum(triple_grad.reshape(fs, cs, wrows, 3 * span).astype(F32), axis=0)
    triple_grad = scatter_sum(triple_grad.astype(BF16), "tensor").astype(BF16)
    triple_grad = gather(triple_grad, "tensor").reshape(cs, wrows, 3, span).astype(F32)
    triple_gradient = jnp.transpose(triple_grad, (1, 2, 0, 3)).reshape(wrows, 3 * width)
    first_gradient = jnp.sum(
        triple_gradient * triple_weight.astype(F32), axis=1
    ) / first_gain.astype(F32)
    return (
        outputs,
        input_gradient,
        first_gradient,
        second_gradient,
        triple_gradient,
        mixing_gradient,
        inner_gradient,
        outer_gradient,
    )


def solution(mesh):
    rows = P("fsdp", ("context", "tensor"), None)
    both = ("fsdp", "context")
    weights = (P(both), P(both), P(both, None), P(both, None), P(both, None, "tensor"), P("tensor", both))
    return jax.shard_map(
        per_device,
        mesh=mesh,
        in_specs=(rows, P("fsdp", None)) + weights + (rows,),
        out_specs=(rows, rows) + weights,
        check_vma=False,
    )
```

```python
import functools

import jax
import jax.numpy as jnp
from jax import lax
from jax.experimental import pallas as pl
from jax.experimental.pallas import tpu as pltpu
from jax.sharding import PartitionSpec as P

H = 12
HD = 64
THETA = 160000.0
EPSILON = 1e-05
MASKED = -1e30
BLOCK = 256
SCALE = HD ** (-0.5)

F32 = jnp.float32
BF16 = jnp.bfloat16


def dot(a, b, ca, cb):
    return lax.dot_general(a, b, (((ca,), (cb,)), ((), ())), preferred_element_type=F32)


def norm_parts(values):
    average = jnp.mean(values, axis=-1, keepdims=True)
    centred = values - average
    variance = jnp.mean(centred * centred, axis=-1, keepdims=True)
    inverse = lax.rsqrt(variance + EPSILON)
    return centred * inverse, inverse


def norm_back(grad, gain, xhat, inverse):
    u = grad * gain
    return inverse * (
        u
        - jnp.mean(u, axis=-1, keepdims=True)
        - xhat * jnp.mean(u * xhat, axis=-1, keepdims=True)
    )


def doc_positions(segments):
    token_index = jnp.arange(segments.shape[-1], dtype=jnp.int32)
    changed = (segments[1:] != segments[:-1]).astype(jnp.int32)
    starts = jnp.concatenate([jnp.ones((1,), jnp.int32), changed], axis=-1)
    return token_index - lax.cummax(token_index * starts, axis=0)


def forward_kernel(heads, lo_ref, hi_ref, q_ref, k_ref, v_ref, qid_ref, kid_ref, o_ref, l_ref):
    b = pl.program_id(0)
    qids = qid_ref[...]
    queries = [q_ref[h] * jnp.asarray(SCALE, BF16) for h in range(heads)]

    def step(j, carry):
        start = pl.multiple_of(j * BLOCK, BLOCK)
        same = kid_ref[pl.ds(start, BLOCK), :] == qids
        new = []
        for h in range(heads):
            peak, total, acc = carry[h]
            s = dot(k_ref[h, :, pl.ds(start, BLOCK)], queries[h], 0, 0)
            s = jnp.where(same, s, MASKED)
            peak_new = jnp.maximum(peak, jnp.max(s, axis=0, keepdims=True))
            fade = jnp.exp(peak - peak_new)
            p = jnp.exp(s - peak_new)
            total = total * fade + jnp.sum(p, axis=0, keepdims=True)
            acc = acc * fade + dot(v_ref[h, :, pl.ds(start, BLOCK)], p.astype(BF16), 1, 0)
            new.append((peak_new, total, acc))
        return tuple(new)

    first = tuple(
        (
            jnp.full((1, BLOCK), MASKED, F32),
            jnp.zeros((1, BLOCK), F32),
            jnp.zeros((HD, BLOCK), F32),
        )
        for _ in range(heads)
    )
    done = lax.fori_loop(lo_ref[b], hi_ref[b], step, first)
    for h in range(heads):
        peak, total, acc = done[h]
        o_ref[0, h] = (acc / total).astype(BF16)
        l_ref[h] = peak + jnp.log(total)


def attention_forward(q, k, v, row_ids, col_ids, lo, hi, parts):
    heads, width, length = q.shape
    per = length // parts // BLOCK
    block = pl.BlockSpec((heads, width, BLOCK), lambda b, *_: (0, 0, b))
    whole = pl.BlockSpec((heads, width, length), lambda b, *_: (0, 0, 0))
    return pl.pallas_call(
        functools.partial(forward_kernel, heads),
        grid_spec=pltpu.PrefetchScalarGridSpec(
            num_scalar_prefetch=2,
            grid=(length // BLOCK,),
            in_specs=[
                block,
                whole,
                whole,
                pl.BlockSpec((1, BLOCK), lambda b, *_: (0, b)),
                pl.BlockSpec((length, 1), lambda b, *_: (0, 0)),
            ],
            out_specs=[
                pl.BlockSpec((1, heads, width, BLOCK), lambda b, *_: (b // per, 0, 0, b % per)),
                pl.BlockSpec((heads, 1, BLOCK), lambda b, *_: (0, 0, b)),
            ],
        ),
        out_shape=[
            jax.ShapeDtypeStruct((parts, heads, width, length // parts), BF16),
            jax.ShapeDtypeStruct((heads, 1, length), F32),
        ],
        compiler_params=pltpu.CompilerParams(vmem_limit_bytes=40 * 1024 * 1024),
        cost_estimate=pl.CostEstimate(
            flops=40 * heads * width * length * length,
            bytes_accessed=10 * heads * width * length,
            transcendentals=heads * length * length // 3,
        ),
        name="attention_forward",
    )(lo, hi, q, k, v, row_ids, col_ids)


def backward_kernel(
    heads, lo_ref, hi_ref, q_ref, do_ref, o_ref, l_ref, k_ref, v_ref, qid_ref, kid_ref,
    dq_ref, dk_ref, dv_ref, dq_sum, row_sum,
):
    b = pl.program_id(0)
    parts, _, _, rows = do_ref.shape
    per = rows // BLOCK

    @pl.when(b == 0)
    def _():
        dq_sum[...] = jnp.zeros_like(dq_sum)
        for c in range(parts):
            for h in range(heads):
                row_sum[h, :, c * rows : (c + 1) * rows] = jnp.sum(
                    do_ref[c, h].astype(F32) * o_ref[c, h].astype(F32), axis=0, keepdims=True
                )

    kids = kid_ref[...]
    scaled = [k_ref[h] * jnp.asarray(SCALE, BF16) for h in range(heads)]
    keys = [s.T for s in scaled]
    values = [v_ref[h].T for h in range(heads)]

    def step(j, carry):
        at = pl.ds(pl.multiple_of(j * BLOCK, BLOCK), BLOCK)
        same = kids == qid_ref[:, at]
        new = []
        for h in range(heads):
            dk, dv = carry[h]
            q = q_ref[h, :, at]
            do = do_ref[j // per, h, :, pl.ds(pl.multiple_of((j % per) * BLOCK, BLOCK), BLOCK)]
            s = dot(keys[h], q, 1, 0)
            s = jnp.where(same, s, MASKED)
            p = jnp.exp(s - l_ref[h, :, at])
            dp = dot(values[h], do, 1, 0)
            ds = (p * (dp - row_sum[h, :, at])).astype(BF16)
            dv = dv + dot(do, p.astype(BF16), 1, 1)
            dk = dk + dot(q, ds, 1, 1)
            dq_sum[h, :, at] += dot(scaled[h], ds, 1, 0)
            new.append((dk, dv))
        return tuple(new)

    zero = jnp.zeros((HD, BLOCK), F32)
    done = lax.fori_loop(lo_ref[b], hi_ref[b], step, tuple((zero, zero) for _ in range(heads)))
    for h in range(heads):
        dk, dv = done[h]
        dk_ref[h] = (dk * SCALE).astype(BF16)
        dv_ref[h] = dv.astype(BF16)

    @pl.when(b == pl.num_programs(0) - 1)
    def _():
        dq_ref[...] = dq_sum[...].astype(BF16)


def attention_backward(q, k, v, o, do, logsum, row_ids, col_ids, lo, hi):
    heads, width, length = q.shape
    block = pl.BlockSpec((heads, width, BLOCK), lambda b, *_: (0, 0, b))
    whole = pl.BlockSpec((heads, width, length), lambda b, *_: (0, 0, 0))
    spread = pl.BlockSpec(do.shape, lambda b, *_: (0, 0, 0, 0))
    shape = jax.ShapeDtypeStruct((heads, width, length), BF16)
    return pl.pallas_call(
        functools.partial(backward_kernel, heads),
        grid_spec=pltpu.PrefetchScalarGridSpec(
            num_scalar_prefetch=2,
            grid=(length // BLOCK,),
            in_specs=[
                whole,
                spread,
                spread,
                pl.BlockSpec((heads, 1, length), lambda b, *_: (0, 0, 0)),
                block,
                block,
                pl.BlockSpec((1, length), lambda b, *_: (0, 0)),
                pl.BlockSpec((BLOCK, 1), lambda b, *_: (b, 0)),
            ],
            out_specs=[whole, block, block],
            scratch_shapes=[
                pltpu.VMEM((heads, width, length), F32),
                pltpu.VMEM((heads, 1, length), F32),
            ],
        ),
        out_shape=[shape, shape, shape],
        compiler_params=pltpu.CompilerParams(vmem_limit_bytes=40 * 1024 * 1024),
        cost_estimate=pl.CostEstimate(
            flops=40 * heads * width * length * length,
            bytes_accessed=16 * heads * width * length,
            transcendentals=heads * length * length // 3,
        ),
        name="attention_backward",
    )(lo, hi, q, do, o, logsum, k, v, row_ids, col_ids)


def gated_unit(gate_part, up_part):
    return jax.nn.gelu(gate_part, approximate=False) * up_part


def turn(values, cosines, sines):
    a, b = values[..., : HD // 2, :], values[..., HD // 2 :, :]
    return jnp.concatenate([a * cosines - b * sines, b * cosines + a * sines], axis=-2)


def gather(block, axis):
    count = lax.axis_size(axis)
    copies = jnp.broadcast_to(block[None], (count,) + block.shape)
    return lax.all_to_all(copies, axis, 0, 0, tiled=True)


def scatter_sum(blocks, axis):
    return jnp.sum(lax.all_to_all(blocks, axis, 0, 0, tiled=True).astype(F32), axis=0)


def per_device(
    tokens, segment_ids, first_gain, second_gain, triple_weight, mixing_weight,
    inner_weight, outer_weight, cotangent,
):
    cs = lax.axis_size("context")
    ts = lax.axis_size("tensor")
    fs = lax.axis_size("fsdp")
    t_rank = lax.axis_index("tensor")
    seqs, rows_in, width = tokens.shape
    assert seqs == ts and ts == cs
    length = segment_ids.shape[1]
    heads = H // cs
    span = heads * HD
    wrows = triple_weight.shape[0]
    units = inner_weight.shape[2]
    rows = rows_in * ts

    own = lax.all_to_all(tokens, "tensor", 0, 0, tiled=True).reshape(rows, width)
    own, triple_late, inner_late, outer_late = lax.optimization_barrier(
        (own, triple_weight, inner_weight, outer_weight)
    )
    every = lax.all_gather(own, "context", axis=0, tiled=True)

    gains = jnp.stack([first_gain, second_gain], axis=1)
    gains = jnp.broadcast_to(jnp.pad(gains, ((0, 0), (0, 62)))[None], (cs, wrows, 64))
    columns = jnp.transpose(triple_late.reshape(wrows, 3, cs, span), (2, 0, 1, 3))
    columns = jnp.concatenate([columns.reshape(cs, wrows, 3 * span), gains], axis=2)
    columns = lax.all_to_all(columns, "context", 0, 0, tiled=True).reshape(cs * wrows, -1)
    columns = gather(columns, "fsdp").reshape(width, -1)
    w_own = columns[:, : 3 * span]
    gain_one = columns[:, 3 * span].astype(F32)
    gain_two = columns[:, 3 * span + 1].astype(F32)

    full = ts * units
    unit_own = jnp.concatenate([inner_late.reshape(wrows, 2 * units), outer_late.T], axis=1)
    unit_all = gather(unit_own, "tensor").reshape(ts, wrows, 3, units)
    unit_all = jnp.transpose(unit_all, (1, 2, 0, 3)).reshape(wrows, 3 * full)
    packed = jnp.concatenate([unit_all, mixing_weight], axis=1)
    packed, every, cotangent = lax.optimization_barrier((packed, every, cotangent))
    packed = lax.all_gather(packed, "context", axis=0, tiled=True)
    residual = own.astype(F32)
    xhat_one, inverse_one = norm_parts(residual)
    normed_one = (norm_parts(every.astype(F32))[0] * gain_one).astype(BF16)
    cot = lax.all_to_all(cotangent, "tensor", 0, 0, tiled=True).reshape(rows, width)

    segments = lax.dynamic_index_in_dim(segment_ids, t_rank, 0, keepdims=False)
    positions = doc_positions(segments)
    freqs = THETA ** (-(jnp.arange(HD // 2, dtype=F32) * (2.0 / HD)))
    angles = freqs[:, None] * positions.astype(F32)[None, :]
    cosines, sines = jnp.cos(angles), jnp.sin(angles)
    by_block = segments.reshape(length // BLOCK, BLOCK)
    low_at = jnp.sum(segments[None, :] < by_block[:, :1], axis=1, dtype=jnp.int32)
    high_at = jnp.sum(segments[None, :] <= by_block[:, -1:], axis=1, dtype=jnp.int32)
    lo = low_at // BLOCK
    hi = (high_at + BLOCK - 1) // BLOCK
    row_ids = segments.reshape(1, length)
    col_ids = segments.reshape(length, 1)

    projected = dot(w_own, normed_one, 0, 1).reshape(3, heads, HD, length)
    q = turn(projected[0], cosines, sines).astype(BF16)
    k = turn(projected[1], cosines, sines).astype(BF16)
    v = projected[2].astype(BF16)
    o, logsum = attention_forward(q, k, v, row_ids, col_ids, lo, hi, cs)

    sent = o.reshape(cs, span, rows)
    attended = lax.all_to_all(sent, "context", 0, 0, tiled=True).reshape(cs * span, rows)

    packed, attended = lax.optimization_barrier((packed, attended))
    packed = gather(packed, "fsdp").reshape(width, 3 * full + width)
    inner = packed[:, : 2 * full]
    outer_t = packed[:, 2 * full : 3 * full]
    mixing = packed[:, 3 * full :]
    middle = residual + dot(attended, mixing, 0, 0)
    xhat_two, inverse_two = norm_parts(middle)
    normed_two = (xhat_two * gain_two).astype(BF16)
    gate_up = dot(normed_two, inner, 1, 0)
    hidden, unit_pull = jax.vjp(gated_unit, gate_up[:, :full], gate_up[:, full:])
    hidden = hidden.astype(BF16)
    outputs = (middle + dot(hidden, outer_t, 1, 1)).astype(BF16)
    grad_hidden = dot(cot, outer_t, 1, 0)
    grad_gate, grad_up = unit_pull(grad_hidden)
    grad_gate_up = jnp.concatenate([grad_gate, grad_up], axis=1).astype(BF16)
    grad_two = dot(grad_gate_up, inner, 1, 1)
    second_part = jnp.sum(grad_two * xhat_two, axis=0)
    grad_middle = cot.astype(F32) + norm_back(grad_two, gain_two, xhat_two, inverse_two)
    grad_mixed = grad_middle.astype(BF16)
    grad_att = dot(mixing, grad_mixed, 1, 1).astype(BF16)
    grad_att = lax.all_to_all(grad_att.reshape(cs, span, rows), "context", 0, 0, tiled=True)
    do = grad_att.reshape(cs, heads, HD, rows)

    second_wide = jnp.broadcast_to(second_part[:, None], (width, 128))
    weight_grad = jnp.concatenate(
        [
            dot(normed_two, grad_gate_up, 0, 0).astype(BF16),
            dot(cot, hidden, 0, 0).astype(BF16),
            dot(attended, grad_mixed, 1, 0).astype(BF16),
            second_wide.astype(BF16),
        ],
        axis=1,
    )
    lanes = 3 * full + width + 128
    weight_grad = lax.all_to_all(
        weight_grad.reshape(fs, cs * wrows, lanes), "fsdp", 0, 0, tiled=True
    )
    outputs = lax.all_to_all(outputs.reshape(ts, rows_in, width), "tensor", 0, 0, tiled=True)

    dq, dk, dv = attention_backward(q, k, v, o, do, logsum, row_ids, col_ids, lo, hi)
    dq, outputs, weight_grad = lax.optimization_barrier((dq, outputs, weight_grad))
    weight_grad = jnp.sum(weight_grad.astype(F32), axis=0).astype(BF16)
    weight_grad = lax.psum_scatter(
        weight_grad.reshape(cs, wrows, lanes), "context", scatter_dimension=0, tiled=True
    )[0]
    unit_grad = jnp.transpose(weight_grad[:, : 3 * full].reshape(wrows, 3, ts, units), (2, 0, 1, 3))
    unit_grad = unit_grad.reshape(ts, wrows, 3 * units)
    unit_grad = lax.psum_scatter(unit_grad, "tensor", scatter_dimension=0, tiled=True)[0]
    unit_grad = unit_grad.astype(F32)
    other_grad = lax.psum(weight_grad[:, 3 * full :], "tensor").astype(F32)
    mixing_gradient = other_grad[:, :width]
    second_gradient = other_grad[:, width]
    inner_gradient = unit_grad[:, : 2 * units].reshape(wrows, 2, units)
    outer_gradient = unit_grad[:, 2 * units :].T

    grad_p = jnp.concatenate(
        [
            turn(dq.astype(F32), cosines, -sines).astype(BF16),
            turn(dk.astype(F32), cosines, -sines).astype(BF16),
            dv,
        ],
        axis=0,
    ).reshape(3 * span, length)
    grad_one = dot(grad_p, w_own, 0, 1).astype(BF16).reshape(cs, rows, width)
    grad_one = lax.all_to_all(grad_one, "context", 0, 0, tiled=True)
    triple_grad = dot(normed_one, grad_p, 0, 1).astype(BF16).reshape(fs * cs, wrows, 3 * span)
    grad_one, triple_grad = lax.optimization_barrier((grad_one, triple_grad))
    grad_one = jnp.sum(grad_one.astype(F32), axis=0)
    input_gradient = grad_middle + norm_back(grad_one, gain_one, xhat_one, inverse_one)
    input_gradient = lax.all_to_all(
        input_gradient.astype(BF16).reshape(ts, rows_in, width), "tensor", 0, 0, tiled=True
    ).astype(F32)

    triple_grad = lax.all_to_all(triple_grad, ("fsdp", "context"), 0, 0, tiled=True)
    triple_grad = jnp.sum(triple_grad.reshape(fs, cs, wrows, 3 * span).astype(F32), axis=0)
    triple_grad = scatter_sum(triple_grad.astype(BF16), "tensor").astype(BF16)
    triple_grad = gather(triple_grad, "tensor").reshape(cs, wrows, 3, span).astype(F32)
    triple_gradient = jnp.transpose(triple_grad, (1, 2, 0, 3)).reshape(wrows, 3 * width)
    first_gradient = jnp.sum(
        triple_gradient * triple_weight.astype(F32), axis=1
    ) / first_gain.astype(F32)
    return (
        outputs,
        input_gradient,
        first_gradient,
        second_gradient,
        triple_gradient,
        mixing_gradient,
        inner_gradient,
        outer_gradient,
    )


def solution(mesh):
    rows = P("fsdp", ("context", "tensor"), None)
    both = ("fsdp", "context")
    weights = (P(both), P(both), P(both, None), P(both, None), P(both, None, "tensor"), P("tensor", both))
    return jax.shard_map(
        per_device,
        mesh=mesh,
        in_specs=(rows, P("fsdp", None)) + weights + (rows,),
        out_specs=(rows, rows) + weights,
        check_vma=False,
    )
```

```python
import functools

import jax
import jax.numpy as jnp
from jax import lax
from jax.experimental import pallas as pl
from jax.experimental.pallas import tpu as pltpu
from jax.sharding import PartitionSpec as P

H = 12
HD = 64
THETA = 160000.0
EPSILON = 1e-05
MASKED = -1e30
BLOCK = 256
SCALE = HD ** (-0.5)

F32 = jnp.float32
BF16 = jnp.bfloat16


def dot(a, b, ca, cb):
    return lax.dot_general(a, b, (((ca,), (cb,)), ((), ())), preferred_element_type=F32)


def norm_parts(values):
    average = jnp.mean(values, axis=-1, keepdims=True)
    centred = values - average
    variance = jnp.mean(centred * centred, axis=-1, keepdims=True)
    inverse = lax.rsqrt(variance + EPSILON)
    return centred * inverse, inverse


def norm_back(grad, gain, xhat, inverse):
    u = grad * gain
    return inverse * (
        u
        - jnp.mean(u, axis=-1, keepdims=True)
        - xhat * jnp.mean(u * xhat, axis=-1, keepdims=True)
    )


def doc_positions(segments):
    token_index = jnp.arange(segments.shape[-1], dtype=jnp.int32)
    changed = (segments[1:] != segments[:-1]).astype(jnp.int32)
    starts = jnp.concatenate([jnp.ones((1,), jnp.int32), changed], axis=-1)
    return token_index - lax.cummax(token_index * starts, axis=0)


def forward_kernel(heads, lo_ref, hi_ref, q_ref, k_ref, v_ref, qid_ref, kid_ref, o_ref, l_ref):
    b = pl.program_id(0)
    qids = qid_ref[...]
    queries = [q_ref[h] * jnp.asarray(SCALE, BF16) for h in range(heads)]

    def step(j, carry):
        start = pl.multiple_of(j * BLOCK, BLOCK)
        same = kid_ref[pl.ds(start, BLOCK), :] == qids
        new = []
        for h in range(heads):
            peak, total, acc = carry[h]
            s = dot(k_ref[h, :, pl.ds(start, BLOCK)], queries[h], 0, 0)
            s = jnp.where(same, s, MASKED)
            peak_new = jnp.maximum(peak, jnp.max(s, axis=0, keepdims=True))
            fade = jnp.exp(peak - peak_new)
            p = jnp.exp(s - peak_new)
            total = total * fade + jnp.sum(p, axis=0, keepdims=True)
            acc = acc * fade + dot(v_ref[h, :, pl.ds(start, BLOCK)], p.astype(BF16), 1, 0)
            new.append((peak_new, total, acc))
        return tuple(new)

    first = tuple(
        (
            jnp.full((1, BLOCK), MASKED, F32),
            jnp.zeros((1, BLOCK), F32),
            jnp.zeros((HD, BLOCK), F32),
        )
        for _ in range(heads)
    )
    done = lax.fori_loop(lo_ref[b], hi_ref[b], step, first)
    for h in range(heads):
        peak, total, acc = done[h]
        o_ref[0, h] = (acc / total).astype(BF16)
        l_ref[h] = peak + jnp.log(total)


def attention_forward(q, k, v, row_ids, col_ids, lo, hi, parts):
    heads, width, length = q.shape
    per = length // parts // BLOCK
    block = pl.BlockSpec((heads, width, BLOCK), lambda b, *_: (0, 0, b))
    whole = pl.BlockSpec((heads, width, length), lambda b, *_: (0, 0, 0))
    return pl.pallas_call(
        functools.partial(forward_kernel, heads),
        grid_spec=pltpu.PrefetchScalarGridSpec(
            num_scalar_prefetch=2,
            grid=(length // BLOCK,),
            in_specs=[
                block,
                whole,
                whole,
                pl.BlockSpec((1, BLOCK), lambda b, *_: (0, b)),
                pl.BlockSpec((length, 1), lambda b, *_: (0, 0)),
            ],
            out_specs=[
                pl.BlockSpec((1, heads, width, BLOCK), lambda b, *_: (b // per, 0, 0, b % per)),
                pl.BlockSpec((heads, 1, BLOCK), lambda b, *_: (0, 0, b)),
            ],
        ),
        out_shape=[
            jax.ShapeDtypeStruct((parts, heads, width, length // parts), BF16),
            jax.ShapeDtypeStruct((heads, 1, length), F32),
        ],
        compiler_params=pltpu.CompilerParams(vmem_limit_bytes=40 * 1024 * 1024),
        cost_estimate=pl.CostEstimate(
            flops=40 * heads * width * length * length,
            bytes_accessed=10 * heads * width * length,
            transcendentals=heads * length * length // 3,
        ),
        name="attention_forward",
    )(lo, hi, q, k, v, row_ids, col_ids)


def backward_kernel(
    heads, lo_ref, hi_ref, q_ref, do_ref, o_ref, l_ref, k_ref, v_ref, qid_ref, kid_ref,
    dq_ref, dk_ref, dv_ref, dq_sum, row_sum,
):
    b = pl.program_id(0)
    parts, _, _, rows = do_ref.shape
    per = rows // BLOCK

    @pl.when(b == 0)
    def _():
        dq_sum[...] = jnp.zeros_like(dq_sum)
        for c in range(parts):
            for h in range(heads):
                row_sum[h, :, c * rows : (c + 1) * rows] = jnp.sum(
                    do_ref[c, h].astype(F32) * o_ref[c, h].astype(F32), axis=0, keepdims=True
                )

    kids = kid_ref[...]
    scaled = [k_ref[h] * jnp.asarray(SCALE, BF16) for h in range(heads)]
    keys = [s.T for s in scaled]
    values = [v_ref[h].T for h in range(heads)]

    def step(j, carry):
        at = pl.ds(pl.multiple_of(j * BLOCK, BLOCK), BLOCK)
        same = kids == qid_ref[:, at]
        new = []
        for h in range(heads):
            dk, dv = carry[h]
            q = q_ref[h, :, at]
            do = do_ref[j // per, h, :, pl.ds(pl.multiple_of((j % per) * BLOCK, BLOCK), BLOCK)]
            s = dot(keys[h], q, 1, 0)
            s = jnp.where(same, s, MASKED)
            p = jnp.exp(s - l_ref[h, :, at])
            dp = dot(values[h], do, 1, 0)
            ds = (p * (dp - row_sum[h, :, at])).astype(BF16)
            dv = dv + dot(do, p.astype(BF16), 1, 1)
            dk = dk + dot(q, ds, 1, 1)
            dq_sum[h, :, at] += dot(scaled[h], ds, 1, 0)
            new.append((dk, dv))
        return tuple(new)

    zero = jnp.zeros((HD, BLOCK), F32)
    done = lax.fori_loop(lo_ref[b], hi_ref[b], step, tuple((zero, zero) for _ in range(heads)))
    for h in range(heads):
        dk, dv = done[h]
        dk_ref[h] = (dk * SCALE).astype(BF16)
        dv_ref[h] = dv.astype(BF16)

    @pl.when(b == pl.num_programs(0) - 1)
    def _():
        dq_ref[...] = dq_sum[...].astype(BF16)


def attention_backward(q, k, v, o, do, logsum, row_ids, col_ids, lo, hi):
    heads, width, length = q.shape
    block = pl.BlockSpec((heads, width, BLOCK), lambda b, *_: (0, 0, b))
    whole = pl.BlockSpec((heads, width, length), lambda b, *_: (0, 0, 0))
    spread = pl.BlockSpec(do.shape, lambda b, *_: (0, 0, 0, 0))
    shape = jax.ShapeDtypeStruct((heads, width, length), BF16)
    return pl.pallas_call(
        functools.partial(backward_kernel, heads),
        grid_spec=pltpu.PrefetchScalarGridSpec(
            num_scalar_prefetch=2,
            grid=(length // BLOCK,),
            in_specs=[
                whole,
                spread,
                spread,
                pl.BlockSpec((heads, 1, length), lambda b, *_: (0, 0, 0)),
                block,
                block,
                pl.BlockSpec((1, length), lambda b, *_: (0, 0)),
                pl.BlockSpec((BLOCK, 1), lambda b, *_: (b, 0)),
            ],
            out_specs=[whole, block, block],
            scratch_shapes=[
                pltpu.VMEM((heads, width, length), F32),
                pltpu.VMEM((heads, 1, length), F32),
            ],
        ),
        out_shape=[shape, shape, shape],
        compiler_params=pltpu.CompilerParams(vmem_limit_bytes=40 * 1024 * 1024),
        cost_estimate=pl.CostEstimate(
            flops=40 * heads * width * length * length,
            bytes_accessed=16 * heads * width * length,
            transcendentals=heads * length * length // 3,
        ),
        name="attention_backward",
    )(lo, hi, q, do, o, logsum, k, v, row_ids, col_ids)


def gated_unit(gate_part, up_part):
    return jax.nn.gelu(gate_part, approximate=False) * up_part


def turn(values, cosines, sines):
    a, b = values[..., : HD // 2, :], values[..., HD // 2 :, :]
    return jnp.concatenate([a * cosines - b * sines, b * cosines + a * sines], axis=-2)


def gather(block, axis):
    count = lax.axis_size(axis)
    copies = jnp.broadcast_to(block[None], (count,) + block.shape)
    return lax.all_to_all(copies, axis, 0, 0, tiled=True)


def scatter_sum(blocks, axis):
    return jnp.sum(lax.all_to_all(blocks, axis, 0, 0, tiled=True).astype(F32), axis=0)


def per_device(
    tokens, segment_ids, first_gain, second_gain, triple_weight, mixing_weight,
    inner_weight, outer_weight, cotangent,
):
    cs = lax.axis_size("context")
    ts = lax.axis_size("tensor")
    fs = lax.axis_size("fsdp")
    t_rank = lax.axis_index("tensor")
    seqs, rows_in, width = tokens.shape
    assert seqs == ts and ts == cs
    length = segment_ids.shape[1]
    heads = H // cs
    span = heads * HD
    wrows = triple_weight.shape[0]
    units = inner_weight.shape[2]
    rows = rows_in * ts

    own = lax.all_to_all(tokens, "tensor", 0, 0, tiled=True).reshape(rows, width)
    own, triple_late, inner_late, outer_late = lax.optimization_barrier(
        (own, triple_weight, inner_weight, outer_weight)
    )
    every = lax.all_gather(own, "context", axis=0, tiled=True)

    gains = jnp.stack([first_gain, second_gain], axis=1)
    gains = jnp.broadcast_to(jnp.pad(gains, ((0, 0), (0, 62)))[None], (cs, wrows, 64))
    columns = jnp.transpose(triple_late.reshape(wrows, 3, cs, span), (2, 0, 1, 3))
    columns = jnp.concatenate([columns.reshape(cs, wrows, 3 * span), gains], axis=2)
    columns = lax.all_to_all(columns, "context", 0, 0, tiled=True).reshape(cs * wrows, -1)
    columns = gather(columns, "fsdp").reshape(width, -1)
    w_own = columns[:, : 3 * span]
    gain_one = columns[:, 3 * span].astype(F32)
    gain_two = columns[:, 3 * span + 1].astype(F32)

    full = ts * units
    unit_own = jnp.concatenate([inner_late.reshape(wrows, 2 * units), outer_late.T], axis=1)
    unit_all = gather(unit_own, "tensor").reshape(ts, wrows, 3, units)
    unit_all = jnp.transpose(unit_all, (1, 2, 0, 3)).reshape(wrows, 3 * full)
    packed = jnp.concatenate([unit_all, mixing_weight], axis=1)
    packed, every, cotangent = lax.optimization_barrier((packed, every, cotangent))
    packed = lax.all_gather(packed, "context", axis=0, tiled=True)
    residual = own.astype(F32)
    xhat_one, inverse_one = norm_parts(residual)
    normed_one = (norm_parts(every.astype(F32))[0] * gain_one).astype(BF16)
    cot = lax.all_to_all(cotangent, "tensor", 0, 0, tiled=True).reshape(rows, width)

    segments = lax.dynamic_index_in_dim(segment_ids, t_rank, 0, keepdims=False)
    positions = doc_positions(segments)
    freqs = THETA ** (-(jnp.arange(HD // 2, dtype=F32) * (2.0 / HD)))
    angles = freqs[:, None] * positions.astype(F32)[None, :]
    cosines, sines = jnp.cos(angles), jnp.sin(angles)
    by_block = segments.reshape(length // BLOCK, BLOCK)
    low_at = jnp.sum(segments[None, :] < by_block[:, :1], axis=1, dtype=jnp.int32)
    high_at = jnp.sum(segments[None, :] <= by_block[:, -1:], axis=1, dtype=jnp.int32)
    lo = low_at // BLOCK
    hi = (high_at + BLOCK - 1) // BLOCK
    row_ids = segments.reshape(1, length)
    col_ids = segments.reshape(length, 1)

    projected = dot(w_own, normed_one, 0, 1).reshape(3, heads, HD, length)
    q = turn(projected[0], cosines, sines).astype(BF16)
    k = turn(projected[1], cosines, sines).astype(BF16)
    v = projected[2].astype(BF16)
    o, logsum = attention_forward(q, k, v, row_ids, col_ids, lo, hi, cs)

    sent = o.reshape(cs, span, rows)
    attended = lax.all_to_all(sent, "context", 0, 0, tiled=True).reshape(cs * span, rows)

    packed, attended = lax.optimization_barrier((packed, attended))
    packed = gather(packed, "fsdp").reshape(width, 3 * full + width)
    inner = packed[:, : 2 * full]
    outer_t = packed[:, 2 * full : 3 * full]
    mixing = packed[:, 3 * full :]
    middle = residual + dot(attended, mixing, 0, 0)
    xhat_two, inverse_two = norm_parts(middle)
    normed_two = (xhat_two * gain_two).astype(BF16)
    gate_up = dot(normed_two, inner, 1, 0)
    hidden, unit_pull = jax.vjp(gated_unit, gate_up[:, :full], gate_up[:, full:])
    hidden = hidden.astype(BF16)
    outputs = (middle + dot(hidden, outer_t, 1, 1)).astype(BF16)
    grad_hidden = dot(cot, outer_t, 1, 0)
    grad_gate, grad_up = unit_pull(grad_hidden)
    grad_gate_up = jnp.concatenate([grad_gate, grad_up], axis=1).astype(BF16)
    grad_two = dot(grad_gate_up, inner, 1, 1)
    second_part = jnp.sum(grad_two * xhat_two, axis=0)
    grad_middle = cot.astype(F32) + norm_back(grad_two, gain_two, xhat_two, inverse_two)
    grad_mixed = grad_middle.astype(BF16)
    grad_att = dot(mixing, grad_mixed, 1, 1).astype(BF16)
    grad_att = lax.all_to_all(grad_att.reshape(cs, span, rows), "context", 0, 0, tiled=True)
    do = grad_att.reshape(cs, heads, HD, rows)

    second_wide = jnp.broadcast_to(second_part[:, None], (width, 128))
    weight_grad = jnp.concatenate(
        [
            dot(normed_two, grad_gate_up, 0, 0).astype(BF16),
            dot(cot, hidden, 0, 0).astype(BF16),
            dot(attended, grad_mixed, 1, 0).astype(BF16),
            second_wide.astype(BF16),
        ],
        axis=1,
    )
    lanes = 3 * full + width + 128
    weight_grad = lax.all_to_all(
        weight_grad.reshape(fs, cs * wrows, lanes), "fsdp", 0, 0, tiled=True
    )
    weight_grad = jnp.sum(weight_grad.astype(F32), axis=0).astype(BF16)
    do, weight_grad, outputs = lax.optimization_barrier((do, weight_grad, outputs))
    weight_grad = lax.psum_scatter(
        weight_grad.reshape(cs, wrows, lanes), "context", scatter_dimension=0, tiled=True
    )[0]
    outputs = lax.all_to_all(outputs.reshape(ts, rows_in, width), "tensor", 0, 0, tiled=True)

    dq, dk, dv = attention_backward(q, k, v, o, do, logsum, row_ids, col_ids, lo, hi)
    dq, outputs = lax.optimization_barrier((dq, outputs))
    grad_p = jnp.concatenate(
        [
            turn(dq.astype(F32), cosines, -sines).astype(BF16),
            turn(dk.astype(F32), cosines, -sines).astype(BF16),
            dv,
        ],
        axis=0,
    ).reshape(3 * span, length)
    grad_one = dot(grad_p, w_own, 0, 1).astype(BF16).reshape(cs, rows, width)
    grad_one = lax.all_to_all(grad_one, "context", 0, 0, tiled=True)
    triple_grad = dot(normed_one, grad_p, 0, 1).astype(BF16).reshape(fs * cs, wrows, 3 * span)
    grad_one, triple_grad = lax.optimization_barrier((grad_one, triple_grad))
    grad_one = jnp.sum(grad_one.astype(F32), axis=0)
    input_gradient = grad_middle + norm_back(grad_one, gain_one, xhat_one, inverse_one)
    input_gradient = lax.all_to_all(
        input_gradient.astype(BF16).reshape(ts, rows_in, width), "tensor", 0, 0, tiled=True
    ).astype(F32)

    triple_grad = lax.all_to_all(triple_grad, ("fsdp", "context"), 0, 0, tiled=True)
    triple_grad = jnp.sum(triple_grad.reshape(fs, cs, wrows, 3 * span).astype(F32), axis=0)
    unit_grad = jnp.transpose(weight_grad[:, : 3 * full].reshape(wrows, 3, ts, units), (2, 0, 1, 3))
    unit_grad = unit_grad.reshape(ts, wrows, 3 * units)
    quarter = (width + 128) // ts
    other_grad = jnp.transpose(weight_grad[:, 3 * full :].reshape(wrows, ts, quarter), (1, 0, 2))
    last = scatter_sum(
        jnp.concatenate([triple_grad.astype(BF16), other_grad, unit_grad], axis=2), "tensor"
    )
    shared = 3 * span + quarter
    unit_grad = last[:, shared:]
    inner_gradient = unit_grad[:, : 2 * units].reshape(wrows, 2, units)
    outer_gradient = unit_grad[:, 2 * units :].T
    last = gather(last[:, :shared].astype(BF16), "tensor").astype(F32)
    other_grad = jnp.transpose(last[:, :, 3 * span :], (1, 0, 2)).reshape(wrows, width + 128)
    mixing_gradient = other_grad[:, :width]
    second_gradient = other_grad[:, width]
    triple_grad = last[:, :, : 3 * span].reshape(cs, wrows, 3, span)
    triple_gradient = jnp.transpose(triple_grad, (1, 2, 0, 3)).reshape(wrows, 3 * width)
    first_gradient = jnp.sum(
        triple_gradient * triple_weight.astype(F32), axis=1
    ) / first_gain.astype(F32)
    return (
        outputs,
        input_gradient,
        first_gradient,
        second_gradient,
        triple_gradient,
        mixing_gradient,
        inner_gradient,
        outer_gradient,
    )


def solution(mesh):
    rows = P("fsdp", ("context", "tensor"), None)
    both = ("fsdp", "context")
    weights = (P(both), P(both), P(both, None), P(both, None), P(both, None, "tensor"), P("tensor", both))
    return jax.shard_map(
        per_device,
        mesh=mesh,
        in_specs=(rows, P("fsdp", None)) + weights + (rows,),
        out_specs=(rows, rows) + weights,
        check_vma=False,
    )
```
